32 devices in a mesh: ga: 2 (over y), col: 16 (over z, x, core).
Axes of the slice: x: 2, y: 2, z: 4, core: 2. Of those that a mesh axis runs over, the one named last changes fastest.
Arguments:
- query_nope: bfloat16 [128, 4096], P(('ga', 'col')), parts along dimension 0, may hold values from -6 to 6
- query_rope: bfloat16 [128, 2048], P(('ga', 'col')), parts along dimension 0, may hold values from -104 to 104, as said below
- cache: bfloat16 [8192, 576], P(('ga', 'col')), parts along dimension 0, may hold values from -6 to 6, as said below
- key_docs: int32 [8192], P(('ga', 'col')), parts along dimension 0, may hold values from 0 to 7, as said below
- query_docs: int32 [128], P(('ga', 'col')), parts along dimension 0, may hold values from 0 to 7, as said below
- query_pos: int32 [128], P(('ga', 'col')), parts along dimension 0, may hold values from 1 to 4095, as said below
- w_uk: bfloat16 [512, 4096], replicated, may hold values from -0.25 to 0.25
- w_uv: bfloat16 [512, 4096], replicated, may hold values from -0.25 to 0.25
Outputs:
- attended: bfloat16 [128, 4096], P(('ga', 'col')), parts along dimension 0
The draws below stay inside these ranges and needn't reach their ends.
There are 2 independent parts, one for each index of `ga`. The reference program is written for one: setup_inputs(seed, part) draws one part's arguments, and reference() takes and returns one part's arrays. A program takes and returns all parts, laid end to end along the dimension named above; an argument that names none is the same for every part. Nothing has to cross between parts.
Inputs may be any that keep to these rules, and one draw needn't show every extreme that they name: `key_docs`: ids start at 0 and never fall along the cache; a document is a run of equal ids; eight documents. query_docs[i] equals key_docs[query_pos[i]]. `query_pos`: a position from 1 to 4095, never the first token of a document. `query_rope`: real values. `cache`: real values.
All inputs are finite; a program needn't handle non-finite values.
Results may differ from the reference program's by a relative error of at most 0.001.
Values may be sent and summed in bfloat16 or wider, within the bound.
A program may use at most 192 MiB of HBM per device.

```python
import math
import jax
import jax.numpy as jnp
from jax import lax

H = 32
DN = 128
DR = 64
DV = 128
R = 512
CACHE = 4096
QUERIES = 64


def layout_ints(key):
    base_key = jax.random.fold_in(key, 11)
    first_key, second_key = jax.random.split(base_key)
    halves = jax.random.permutation(first_key, CACHE // 2 - 1)[:7].astype(jnp.int32)
    bounds = 2 * (halves + 1)
    flags = jnp.zeros((CACHE,), jnp.int32).at[bounds].set(1)
    documents = jnp.cumsum(flags).astype(jnp.int32)
    positions = jax.random.randint(second_key, (QUERIES,), 1, CACHE).astype(jnp.int32)
    positions = jnp.where(flags[positions] == 1, positions - 1, positions).astype(jnp.int32)
    positions = positions.at[0].set(CACHE - 1)
    positions = positions.at[1].set(1)
    return (documents, positions, documents[positions])


def float_parts(key):
    float_key = jax.random.fold_in(key, 23)
    cache_key, rope_key = jax.random.split(float_key)
    table = jnp.clip(jax.random.normal(cache_key, (CACHE, R + DR), jnp.float32), -6.0, 6.0)
    turned = jnp.clip(jax.random.normal(rope_key, (QUERIES, H * DR), jnp.float32), -6.0, 6.0)
    return (table, turned)


def draw_cache(key, part):
    return float_parts(key)[0].astype(jnp.bfloat16)


def draw_query_rope(key, part):
    return float_parts(key)[1].astype(jnp.bfloat16)


def draw_key_docs(key, part):
    return layout_ints(key)[0]


def draw_query_pos(key, part):
    return layout_ints(key)[1]


def draw_query_docs(key, part):
    return layout_ints(key)[2]


def block_scale(stream_key, shape, shards, low, high):
    def one(dim, blocks):
        heights = jax.random.uniform(jax.random.fold_in(jax.random.fold_in(stream_key, 6), dim), (blocks,), jnp.float32, low / len(shards), high / len(shards))
        return jnp.repeat(jnp.exp(heights), shape[dim] // blocks).reshape((-1,) + (1,) * (len(shape) - dim - 1))

    loudness = one(*shards[0])
    for cut in shards[1:]:
        loudness = loudness * one(*cut)
    return loudness


def noise(own_key, extent, scale, limit, shards=(), kind=jnp.bfloat16):
    drawn = jax.random.normal(own_key, extent, jnp.float32) * scale
    if len(shards) > 0:
        drawn = block_scale(own_key, extent, shards, -0.22, 0.18) * drawn
    return jnp.clip(drawn, min=-limit, max=limit).astype(kind)


def setup_inputs(seed: int = 0, part: int = 0) -> dict:
    seeds = jax.random.split(jax.random.key(seed), 9)
    part_splits = jax.random.split(jax.random.fold_in(seeds[8], part), 9)
    query_nope = noise(part_splits[0], (QUERIES, H * DN), 1.0, 6.0, ((0, 16),))
    query_rope = draw_query_rope(jax.random.fold_in(jax.random.fold_in(seeds[8], part), 71), part)
    cache = draw_cache(jax.random.fold_in(jax.random.fold_in(seeds[8], part), 71), part)
    key_docs = draw_key_docs(jax.random.fold_in(jax.random.fold_in(seeds[8], part), 71), part)
    query_docs = draw_query_docs(jax.random.fold_in(jax.random.fold_in(seeds[8], part), 71), part)
    query_pos = draw_query_pos(jax.random.fold_in(jax.random.fold_in(seeds[8], part), 71), part)
    w_uk = noise(seeds[6], (R, H * DN), R ** -0.5, 0.25)
    w_uv = noise(seeds[7], (R, H * DV), R ** -0.5, 0.25)
    return dict(query_nope=query_nope, query_rope=query_rope, cache=cache, key_docs=key_docs, query_docs=query_docs, query_pos=query_pos, w_uk=w_uk, w_uv=w_uv)


def reference(query_nope, query_rope, cache, key_docs, query_docs, query_pos, w_uk, w_uv):
    scale = 1.0 / math.sqrt(DN + DR)
    highest = lax.Precision.HIGHEST
    latent = cache[:, :R].astype(jnp.float32)
    krope = cache[:, R:].astype(jnp.float32)
    key_place = jnp.arange(CACHE, dtype=jnp.int32)
    visible = (key_docs[None, :] == query_docs[:, None]) & (key_place[None, :] <= query_pos[:, None])
    wide_keys = w_uk.astype(jnp.float32)
    wide_vals = w_uv.astype(jnp.float32)
    q_nope_all = query_nope.astype(jnp.float32)
    q_rope_all = query_rope.astype(jnp.float32)

    def one_head(head):
        w_key = lax.dynamic_slice_in_dim(wide_keys, (head * DN).astype(jnp.int32), DN, 1)
        w_val = lax.dynamic_slice_in_dim(wide_vals, (head * DV).astype(jnp.int32), DV, 1)
        keys = jnp.dot(latent, w_key, precision=highest)
        values = jnp.dot(latent, w_val, precision=highest)
        q_flat = lax.dynamic_slice_in_dim(q_nope_all, (head * DN).astype(jnp.int32), DN, 1)
        q_turn = lax.dynamic_slice_in_dim(q_rope_all, (head * DR).astype(jnp.int32), DR, 1)
        scores = jnp.dot(q_flat, keys.T, precision=highest)
        scores = (scores + jnp.dot(q_turn, krope.T, precision=highest)) * scale
        scores = jnp.where(visible, scores, -1e+30)
        top = lax.optimization_barrier(jnp.max(scores, axis=1, keepdims=True))
        weights = jnp.where(visible, jnp.exp(scores - top), 0.0)
        numer = jnp.dot(weights, values, precision=highest)
        return numer / lax.optimization_barrier(jnp.sum(weights, axis=1, keepdims=True))
    result = lax.map(one_head, jnp.arange(H, dtype=jnp.int32))
    return result.transpose(1, 0, 2).reshape(QUERIES, H * DV).astype(jnp.bfloat16)
```

```python
import functools
import math

import jax
import jax.numpy as jnp
from jax import lax
from jax.experimental import pallas as pl
from jax.experimental.pallas import tpu as pltpu
from jax.sharding import PartitionSpec as P

H = 32
DN = 128
DR = 64
DV = 128
R = 512
PLANE = 4
QUARTERS = 4
STEPS = H // QUARTERS
CHUNKS = 2
MESH = pl.DeviceIdType.MESH
F32 = jnp.float32
BF16 = jnp.bfloat16


def cut(rows):
    units = rows // 16
    ends = [16 * (units * i // CHUNKS) for i in range(CHUNKS + 1)]
    return [(a, b - a) for a, b in zip(ends[:-1], ends[1:])]


def split(x):
    high = x.astype(BF16)
    return high, (x - high.astype(F32)).astype(BF16)


def kernel(
    zs, batches, nope_ref, rope_ref, cache_ref, kdocs_ref, qdocs_ref, qpos_ref, wuk_hbm, wuv_hbm, out_ref,
    wuk, wuv, kbuf, qtmp, qbuf, abuf, sbuf, pbuf, accb, obuf, rbuf,
    wsem, csend, crecv, xsend, xrecv, fsend, frecv, qsend, qrecv, osend, orecv,
):
    me = lax.axis_index("col")
    t = lax.rem(me, PLANE)
    zi = lax.div(me, PLANE)
    base = me - t
    mate_t = t + 1 - 2 * lax.rem(t, 2)
    cross_t = t + 2 - 4 * lax.div(t, 2)
    far_t = mate_t + 2 - 4 * lax.div(mate_t, 2)
    mate, cross = base + mate_t, base + cross_t
    peers = [lax.rem(zi + d, zs) * PLANE + t for d in range(zs)]

    barrier = pltpu.get_barrier_semaphore()
    for other in [mate, cross] + peers[1:]:
        pl.semaphore_signal(barrier, inc=1, device_id={"col": other}, device_id_type=MESH)

    load_uk = pltpu.make_async_copy(wuk_hbm, wuk, wsem.at[0])
    load_uv = pltpu.make_async_copy(wuv_hbm, wuv, wsem.at[1])
    load_uk.start()
    load_uv.start()

    tokens = cache_ref.shape[0]
    own = nope_ref.shape[0]
    rows = QUARTERS * own
    wide = STEPS * DN
    turn = STEPS * DR
    kbuf[0, :tokens, :R] = cache_ref[:, :R]
    krope = cache_ref[:, R:].astype(F32)
    kbuf[0, :tokens, R:] = jnp.concatenate([krope, krope], axis=1).astype(BF16)
    kbuf[0, tokens:, :tokens] = jnp.broadcast_to(kdocs_ref[...].astype(F32), (16, tokens)).astype(BF16)
    kbuf[0, tokens:, tokens:] = jnp.zeros((16, R + 2 * DR - tokens), BF16)
    nope = nope_ref[...].astype(F32)
    rope = rope_ref[...].astype(F32)
    for k in range(QUARTERS):
        qtmp[pl.ds(own * k, own), :wide] = nope[:, k * wide:(k + 1) * wide]
        qtmp[pl.ds(own * k, own), wide:wide + turn] = rope[:, k * turn:(k + 1) * turn]
    row_query = lax.broadcasted_iota(jnp.int32, (rows, 128), 0) % own
    lane = lax.broadcasted_iota(jnp.int32, (rows, 128), 1)
    meta = jnp.zeros((rows, 128), jnp.int32)
    for i in range(own):
        place = qpos_ref[i]
        told = jnp.where(lane == 0, qdocs_ref[i], jnp.where(lane == 1, place >> 7, place & 127))
        meta = jnp.where(row_query == i, told, meta)
    qtmp[:, wide + turn:] = meta.astype(F32)
    qbuf[zi] = qtmp[...].astype(BF16)

    pl.semaphore_wait(barrier, 1 + zs)

    def remote(src, dst, send, recv, to):
        return pltpu.make_async_remote_copy(
            src_ref=src, dst_ref=dst, send_sem=send, recv_sem=recv, device_id={"col": to}, device_id_type=MESH
        )

    pieces = cut(tokens + 16)
    x_copies = [
        remote(kbuf.at[0, pl.ds(a, n)], kbuf.at[2, pl.ds(a, n)], xsend.at[i], xrecv.at[i], cross)
        for i, (a, n) in enumerate(pieces)
    ]
    relays = [
        remote(kbuf.at[2, pl.ds(a, n)], kbuf.at[3, pl.ds(a, n)], fsend.at[i], frecv.at[i], mate)
        for i, (a, n) in enumerate(pieces)
    ]
    q_copies = [remote(qbuf.at[zi], qbuf.at[zi], qsend.at[d], qrecv.at[d], peers[d]) for d in range(1, zs)]
    mate_copy = remote(kbuf.at[0], kbuf.at[1], csend.at[0], crecv.at[0], mate)
    for c in x_copies:
        c.start()
    for c in q_copies:
        c.start()
    mate_copy.start()

    high_rows = zs * rows
    steps = STEPS // batches
    batch_rows = steps * high_rows
    quarter = lax.broadcasted_iota(jnp.int32, (high_rows, 128), 0) % rows // own
    pick = [quarter == k for k in range(QUARTERS)]
    pick_low = [jnp.where(p, 1.0, 0.0).astype(BF16) for p in pick]
    parity = lax.broadcasted_iota(jnp.int32, (high_rows, 128), 1) // DR
    side = [jnp.where(parity == i, 1.0, 0.0).astype(BF16) for i in range(2)]

    for c in q_copies:
        c.wait_recv()
    load_uk.wait()
    for h in range(STEPS):
        b, j = h // steps, h % steps
        q = qbuf[:, :, h * DN:(h + 1) * DN].reshape(high_rows, DN)
        spread = jnp.concatenate([q * p for p in pick_low], axis=1)
        w = jnp.concatenate([wuk[:, k * wide + h * DN:k * wide + (h + 1) * DN] for k in range(QUARTERS)], axis=1)
        absorbed = lax.dot_general(spread, w, (((1,), (1,)), ((), ())), preferred_element_type=F32)
        high, low = split(absorbed)
        at = wide + (h // 2) * 2 * DR
        turned = qbuf[:, :, at:at + 2 * DR].reshape(high_rows, 2 * DR) * side[h % 2]
        span = pl.ds(j * high_rows, high_rows)
        abuf[b, 0, span, :R] = high
        abuf[b, 1, span, :R] = low
        abuf[b, 0, span, R:] = turned
        abuf[b, 1, span, R:] = jnp.zeros_like(turned)

    told = qbuf[:, :, wide + turn:].reshape(high_rows, 128).astype(F32)
    q_doc = told[:, 0:1]
    q_place = told[:, 1:2] * 128.0 + told[:, 2:3]
    factor = math.log2(math.e) / math.sqrt(DN + DR)

    def score(slot, piece_t):
        k_doc = kbuf[slot, tokens:, :tokens].astype(F32)[0:1]
        first = (base + piece_t) * tokens
        k_place = (lax.broadcasted_iota(jnp.int32, (1, tokens), 1) + first).astype(F32)
        visible = (k_doc == q_doc) & (k_place <= q_place)
        keys = kbuf[slot, :tokens, :]
        for b in range(batches):
            both = lax.dot_general(
                abuf[b].reshape(2 * batch_rows, R + 2 * DR), keys, (((1,), (1,)), ((), ())),
                preferred_element_type=F32,
            )
            for j in range(steps):
                a = j * high_rows
                s = (both[a:a + high_rows] + both[batch_rows + a:batch_rows + a + high_rows]) * factor
                sbuf[b, pl.ds(a, high_rows), slot * tokens:(slot + 1) * tokens] = jnp.where(visible, s, -1e30)

    score(0, t)
    mate_copy.wait_recv()
    score(1, mate_t)
    for c, f in zip(x_copies, relays):
        c.wait_recv()
        f.start()
    score(2, cross_t)
    for f in relays:
        f.wait_recv()
    score(3, far_t)

    stat_lane = lax.broadcasted_iota(jnp.int32, (high_rows, 128), 1)
    o_copies = []
    for b in range(batches):
        stats = jnp.zeros((high_rows, 128), F32)
        for j in range(steps):
            span = pl.ds(j * high_rows, high_rows)
            s = sbuf[b, span, :]
            top = jnp.max(s, axis=1, keepdims=True)
            p = jnp.exp2(s - top)
            total = jnp.sum(p, axis=1, keepdims=True)
            high, low = split(p)
            pbuf[0, span, :] = high
            pbuf[1, span, :] = low
            stats = jnp.where(stat_lane == j, top, jnp.where(stat_lane == 64 + j, total, stats))
        probs = pbuf[...].reshape(2 * batch_rows, PLANE * tokens)
        mixed = jnp.dot(
            probs, kbuf[:, :tokens, :R].reshape(PLANE * tokens, R), preferred_element_type=F32
        )
        accb[...] = mixed[:batch_rows] + mixed[batch_rows:]
        if b == 0:
            load_uv.wait()
        for j in range(steps):
            h = b * steps + j
            high, low = split(accb[pl.ds(j * high_rows, high_rows), :])
            w = jnp.concatenate([wuv[:, k * wide + h * DV:k * wide + (h + 1) * DV] for k in range(QUARTERS)], axis=1)
            up = jnp.dot(jnp.concatenate([high, low], axis=0), w, preferred_element_type=F32)
            up = up[:high_rows] + up[high_rows:]
            mine = jnp.zeros((high_rows, DV), F32)
            for k in range(QUARTERS):
                mine = jnp.where(pick[k], up[:, k * DV:(k + 1) * DV], mine)
            obuf[b, :, :, j * DV:(j + 1) * DV] = mine.reshape(zs, rows, DV)
        obuf[b, :, :, steps * DV:] = stats.reshape(zs, rows, 128)
        for d in range(1, zs):
            to = lax.rem(zi + d, zs)
            c = remote(obuf.at[b, to], rbuf.at[b, d], osend.at[b, d], orecv.at[b, d], peers[d])
            c.start()
            o_copies.append(c)

    for b in range(batches):
        for c in o_copies[b * (zs - 1):(b + 1) * (zs - 1)]:
            c.wait_recv()
        mine = obuf[b, zi]
        found = [mine] + [rbuf[b, d] for d in range(1, zs)]
        stats = [f[:, steps * DV:] for f in found]
        top = functools.reduce(jnp.maximum, stats)
        share = [jnp.exp2(s - top) for s in stats]
        for j in range(steps):
            numer = jnp.zeros((rows, DV), F32)
            denom = jnp.zeros((rows, 1), F32)
            for f, s, w in zip(found, stats, share):
                part = w[:, j:j + 1]
                numer += part * f[:, j * DV:(j + 1) * DV]
                denom += part * s[:, 64 + j:65 + j]
            out_ref[:, (b * steps + j) * DV:(b * steps + j + 1) * DV] = numer / denom

    for c in [mate_copy] + x_copies + relays + q_copies + o_copies:
        c.wait_send()


def solution(mesh):
    zs = mesh.shape["col"] // PLANE
    batches = 2 if zs <= 8 else 8
    steps = STEPS // batches

    def shards(query_nope, query_rope, cache, key_docs, query_docs, query_pos, w_uk, w_uv):
        own = query_nope.shape[0]
        rows = QUARTERS * own
        tokens = cache.shape[0]
        payload = STEPS * (DN + DR) + 128
        high_rows = zs * rows
        batch_rows = steps * high_rows
        sem = pltpu.SemaphoreType.DMA
        vmem = pl.BlockSpec(memory_space=pltpu.VMEM)
        smem = pl.BlockSpec(memory_space=pltpu.SMEM)
        hbm = pl.BlockSpec(memory_space=pl.ANY)
        out = pl.pallas_call(
            functools.partial(kernel, zs, batches),
            out_shape=jax.ShapeDtypeStruct((rows, STEPS * DV), F32),
            in_specs=[vmem, vmem, vmem, vmem, smem, smem, hbm, hbm],
            out_specs=vmem,
            scratch_shapes=[
                pltpu.VMEM(w_uk.shape, BF16),
                pltpu.VMEM(w_uv.shape, BF16),
                pltpu.VMEM((PLANE, tokens + 16, R + 2 * DR), BF16),
                pltpu.VMEM((rows, payload), F32),
                pltpu.VMEM((zs, rows, payload), BF16),
                pltpu.VMEM((batches, 2, batch_rows, R + 2 * DR), BF16),
                pltpu.VMEM((batches, batch_rows, PLANE * tokens), F32),
                pltpu.VMEM((2, batch_rows, PLANE * tokens), BF16),
                pltpu.VMEM((batch_rows, R), F32),
                pltpu.VMEM((batches, zs, rows, steps * DV + 128), F32),
                pltpu.VMEM((batches, zs, rows, steps * DV + 128), F32),
                sem((2,)),
                sem((1,)),
                sem((1,)),
                sem((CHUNKS,)),
                sem((CHUNKS,)),
                sem((CHUNKS,)),
                sem((CHUNKS,)),
                sem((zs,)),
                sem((zs,)),
                sem((batches, zs)),
                sem((batches, zs)),
            ],
            compiler_params=pltpu.CompilerParams(
                collective_id=0, has_side_effects=True, vmem_limit_bytes=60 * 1024 * 1024
            ),
        )(query_nope, query_rope, cache, key_docs.reshape(1, tokens), query_docs, query_pos, w_uk, w_uv)
        out = out.reshape(QUARTERS, own, STEPS * DV).transpose(1, 0, 2)
        return out.reshape(own, H * DV).astype(BF16)

    shared = P(("ga", "col"), None)
    flat = P(("ga", "col"))
    return jax.shard_map(
        shards,
        mesh=mesh,
        in_specs=(shared, shared, shared, flat, flat, flat, P(), P()),
        out_specs=shared,
        check_vma=False,
    )
```

```python
import functools
import math

import jax
import jax.numpy as jnp
from jax import lax
from jax.experimental import pallas as pl
from jax.experimental.pallas import tpu as pltpu
from jax.sharding import PartitionSpec as P

H = 32
DN = 128
DR = 64
DV = 128
R = 512
PLANE = 4
QUARTERS = 4
STEPS = H // QUARTERS
CHUNKS = 2
MESH = pl.DeviceIdType.MESH
F32 = jnp.float32
BF16 = jnp.bfloat16


def cut(rows):
    units = rows // 16
    ends = [16 * (units * i // CHUNKS) for i in range(CHUNKS + 1)]
    return [(a, b - a) for a, b in zip(ends[:-1], ends[1:])]


def split(x):
    high = x.astype(BF16)
    return high, (x - high.astype(F32)).astype(BF16)


def kernel(
    zs, batches, groups, nope_ref, rope_ref, cache_ref, kdocs_ref, qdocs_ref, qpos_ref, wuk_hbm, wuv_hbm, out_ref,
    wuk, wuv, kbuf, qtmp, qbuf, abuf, sbuf, pbuf, accb, obuf, rbuf, tbuf, trbuf,
    wsem, csend, crecv, xsend, xrecv, fsend, frecv, qsend, qrecv, osend, orecv, tsend, trecv,
):
    me = lax.axis_index("col")
    t = lax.rem(me, PLANE)
    zi = lax.div(me, PLANE)
    base = me - t
    mate_t = t + 1 - 2 * lax.rem(t, 2)
    cross_t = t + 2 - 4 * lax.div(t, 2)
    far_t = mate_t + 2 - 4 * lax.div(mate_t, 2)
    mate, cross = base + mate_t, base + cross_t
    peers = [lax.rem(zi + d, zs) * PLANE + t for d in range(zs)]

    barrier = pltpu.get_barrier_semaphore()
    for other in [mate, cross] + peers[1:]:
        pl.semaphore_signal(barrier, inc=1, device_id={"col": other}, device_id_type=MESH)

    load_uk = pltpu.make_async_copy(wuk_hbm, wuk, wsem.at[0])
    load_uv = pltpu.make_async_copy(wuv_hbm, wuv, wsem.at[1])
    load_uk.start()
    load_uv.start()

    tokens = cache_ref.shape[1]
    own = nope_ref.shape[0]
    rows = QUARTERS * own
    wide = STEPS * DN
    turn = STEPS * DR
    kbuf[0, :R + DR] = cache_ref[...]
    kbuf[0, R + DR:] = jnp.broadcast_to(kdocs_ref[...].astype(F32), (16, tokens)).astype(BF16)
    nope = nope_ref[...].astype(F32)
    rope = rope_ref[...].astype(F32)
    for k in range(QUARTERS):
        qtmp[pl.ds(own * k, own), :wide] = nope[:, k * wide:(k + 1) * wide]
        qtmp[pl.ds(own * k, own), wide:wide + turn] = rope[:, k * turn:(k + 1) * turn]
    row_query = lax.broadcasted_iota(jnp.int32, (rows, 128), 0) % own
    lane = lax.broadcasted_iota(jnp.int32, (rows, 128), 1)
    meta = jnp.zeros((rows, 128), jnp.int32)
    for i in range(own):
        place = qpos_ref[i]
        told = jnp.where(lane == 0, qdocs_ref[i], jnp.where(lane == 1, place >> 7, place & 127))
        meta = jnp.where(row_query == i, told, meta)
    qtmp[:, wide + turn:] = meta.astype(F32)
    qbuf[zi] = qtmp[...].astype(BF16)

    pl.semaphore_wait(barrier, 1 + zs)

    def remote(src, dst, send, recv, to):
        return pltpu.make_async_remote_copy(
            src_ref=src, dst_ref=dst, send_sem=send, recv_sem=recv, device_id={"col": to}, device_id_type=MESH
        )

    pieces = cut(R + DR + 16)
    x_copies = [
        remote(kbuf.at[0, pl.ds(a, n)], kbuf.at[2, pl.ds(a, n)], xsend.at[i], xrecv.at[i], cross)
        for i, (a, n) in enumerate(pieces)
    ]
    relays = [
        remote(kbuf.at[2, pl.ds(a, n)], kbuf.at[3, pl.ds(a, n)], fsend.at[i], frecv.at[i], mate)
        for i, (a, n) in enumerate(pieces)
    ]
    q_copies = [remote(qbuf.at[zi], qbuf.at[zi], qsend.at[d], qrecv.at[d], peers[d]) for d in range(1, zs)]
    mate_copy = remote(kbuf.at[0], kbuf.at[1], csend.at[0], crecv.at[0], mate)
    for c in x_copies:
        c.start()
    for c in q_copies:
        c.start()
    mate_copy.start()

    high_rows = zs * rows
    steps = STEPS // batches
    batch_rows = steps * high_rows
    group_steps = STEPS // groups
    group_rows = group_steps * high_rows
    quarter = lax.broadcasted_iota(jnp.int32, (high_rows, 128), 0) % rows // own
    pick = [quarter == k for k in range(QUARTERS)]
    pick_low = [jnp.where(p, 1.0, 0.0).astype(BF16) for p in pick]
    parity = lax.broadcasted_iota(jnp.int32, (high_rows, 128), 1) // DR
    side = [jnp.where(parity == i, 1.0, 0.0).astype(BF16) for i in range(2)]

    for c in q_copies:
        c.wait_recv()
    load_uk.wait()
    for h in range(STEPS):
        g, j = h // group_steps, h % group_steps
        q = qbuf[:, :, h * DN:(h + 1) * DN].reshape(high_rows, DN)
        spread = jnp.concatenate([q * p for p in pick_low], axis=1)
        w = jnp.concatenate([wuk[:, k * wide + h * DN:k * wide + (h + 1) * DN] for k in range(QUARTERS)], axis=1)
        absorbed = lax.dot_general(spread, w, (((1,), (1,)), ((), ())), preferred_element_type=F32)
        high, low = split(absorbed)
        at = wide + (h // 2) * 2 * DR
        turned = qbuf[:, :, at:at + 2 * DR].reshape(high_rows, 2 * DR) * side[h % 2]
        span = pl.ds(j * high_rows, high_rows)
        abuf[g, 0, span, :R] = high
        abuf[g, 1, span, :R] = low
        abuf[g, 0, span, R:] = turned
        abuf[g, 1, span, R:] = jnp.zeros_like(turned)

    told = qbuf[:, :, wide + turn:].reshape(high_rows, 128).astype(F32)
    q_doc = told[:, 0:1]
    q_place = told[:, 1:2] * 128.0 + told[:, 2:3]
    factor = math.log2(math.e) / math.sqrt(DN + DR)

    def score(slot, piece_t):
        k_doc = kbuf[slot, R + DR:, :].astype(F32)[0:1]
        first = (base + piece_t) * tokens
        k_place = (lax.broadcasted_iota(jnp.int32, (1, tokens), 1) + first).astype(F32)
        visible = (k_doc == q_doc) & (k_place <= q_place)
        keys = jnp.concatenate([kbuf[slot, :R + DR], kbuf[slot, R:R + DR]], axis=0)
        for g in range(groups):
            both = jnp.dot(abuf[g].reshape(2 * group_rows, R + 2 * DR), keys, preferred_element_type=F32)
            for j in range(group_steps):
                a = j * high_rows
                s = (both[a:a + high_rows] + both[group_rows + a:group_rows + a + high_rows]) * factor
                sbuf[g * group_steps + j, :, slot * tokens:(slot + 1) * tokens] = jnp.where(visible, s, -1e30)

    score(0, t)
    mate_copy.wait_recv()
    score(1, mate_t)
    for c, f in zip(x_copies, relays):
        c.wait_recv()
        f.start()
    score(2, cross_t)
    for f in relays:
        f.wait_recv()
    score(3, far_t)

    stat_lane = lax.broadcasted_iota(jnp.int32, (high_rows, 128), 1)
    o_copies = []
    t_copies = []
    stats = jnp.zeros((high_rows, 128), F32)
    for b in range(batches):
        for j in range(steps):
            span = pl.ds(j * high_rows, high_rows)
            h = b * steps + j
            s = sbuf[h]
            top = jnp.max(s, axis=1, keepdims=True)
            p = jnp.exp2(s - top)
            total = jnp.sum(p, axis=1, keepdims=True)
            high, low = split(p)
            pbuf[0, span, :] = high
            pbuf[1, span, :] = low
            stats = jnp.where(stat_lane == h, top, jnp.where(stat_lane == 64 + h, total, stats))
        if b == batches - 1:
            tbuf[...] = stats.reshape(zs, rows, 128)
            for d in range(1, zs):
                to = lax.rem(zi + d, zs)
                c = remote(tbuf.at[to], trbuf.at[d], tsend.at[d], trecv.at[d], peers[d])
                c.start()
                t_copies.append(c)
        mixed = jnp.zeros((2 * batch_rows, R), F32)
        for slot in range(PLANE):
            probs = pbuf[:, :, slot * tokens:(slot + 1) * tokens].reshape(2 * batch_rows, tokens)
            mixed += lax.dot_general(
                probs, kbuf[slot, :R], (((1,), (1,)), ((), ())), preferred_element_type=F32
            )
        accb[...] = mixed[:batch_rows] + mixed[batch_rows:]
        if b == 0:
            load_uv.wait()
        for j in range(steps):
            h = b * steps + j
            high, low = split(accb[pl.ds(j * high_rows, high_rows), :])
            w = jnp.concatenate([wuv[:, k * wide + h * DV:k * wide + (h + 1) * DV] for k in range(QUARTERS)], axis=1)
            up = jnp.dot(jnp.concatenate([high, low], axis=0), w, preferred_element_type=F32)
            up = up[:high_rows] + up[high_rows:]
            mine = jnp.zeros((high_rows, DV), F32)
            for k in range(QUARTERS):
                mine = jnp.where(pick[k], up[:, k * DV:(k + 1) * DV], mine)
            obuf[b, :, :, j * DV:(j + 1) * DV] = mine.reshape(zs, rows, DV)
        for d in range(1, zs):
            to = lax.rem(zi + d, zs)
            c = remote(obuf.at[b, to], rbuf.at[b, d], osend.at[b, d], orecv.at[b, d], peers[d])
            c.start()
            o_copies.append(c)

    for c in t_copies:
        c.wait_recv()
    stats = [tbuf[zi]] + [trbuf[d] for d in range(1, zs)]
    top = functools.reduce(jnp.maximum, stats)
    share = [jnp.exp2(f - top) for f in stats]
    for b in range(batches):
        for c in o_copies[b * (zs - 1):(b + 1) * (zs - 1)]:
            c.wait_recv()
        found = [obuf[b, zi]] + [rbuf[b, d] for d in range(1, zs)]
        for j in range(steps):
            h = b * steps + j
            numer = jnp.zeros((rows, DV), F32)
            denom = jnp.zeros((rows, 1), F32)
            for f, s, w in zip(found, stats, share):
                part = w[:, h:h + 1]
                numer += part * f[:, j * DV:(j + 1) * DV]
                denom += part * s[:, 64 + h:65 + h]
            done = numer / denom
            for k in range(QUARTERS):
                out_ref[:, k * wide + h * DV:k * wide + (h + 1) * DV] = done[k * own:(k + 1) * own]

    for c in [mate_copy] + x_copies + relays + q_copies + o_copies + t_copies:
        c.wait_send()


def solution(mesh):
    zs = mesh.shape["col"] // PLANE
    batches = 4 if zs <= 8 else 8
    groups = 1 if zs <= 8 else 8
    steps = STEPS // batches

    def shards(query_nope, query_rope, cache, key_docs, query_docs, query_pos, w_uk, w_uv):
        own = query_nope.shape[0]
        rows = QUARTERS * own
        tokens = cache.shape[0]
        payload = STEPS * (DN + DR) + 128
        high_rows = zs * rows
        batch_rows = steps * high_rows
        sem = pltpu.SemaphoreType.DMA
        vmem = pl.BlockSpec(memory_space=pltpu.VMEM)
        smem = pl.BlockSpec(memory_space=pltpu.SMEM)
        hbm = pl.BlockSpec(memory_space=pl.ANY)
        out = pl.pallas_call(
            functools.partial(kernel, zs, batches, groups),
            out_shape=jax.ShapeDtypeStruct((own, H * DV), F32),
            in_specs=[vmem, vmem, vmem, vmem, smem, smem, hbm, hbm],
            out_specs=vmem,
            scratch_shapes=[
                pltpu.VMEM(w_uk.shape, BF16),
                pltpu.VMEM(w_uv.shape, BF16),
                pltpu.VMEM((PLANE, R + DR + 16, tokens), BF16),
                pltpu.VMEM((rows, payload), F32),
                pltpu.VMEM((zs, rows, payload), BF16),
                pltpu.VMEM((groups, 2, STEPS // groups * high_rows, R + 2 * DR), BF16),
                pltpu.VMEM((STEPS, high_rows, PLANE * tokens), F32),
                pltpu.VMEM((2, batch_rows, PLANE * tokens), BF16),
                pltpu.VMEM((batch_rows, R), F32),
                pltpu.VMEM((batches, zs, rows, steps * DV), F32),
                pltpu.VMEM((batches, zs, rows, steps * DV), F32),
                pltpu.VMEM((zs, rows, 128), F32),
                pltpu.VMEM((zs, rows, 128), F32),
                sem((2,)),
                sem((1,)),
                sem((1,)),
                sem((CHUNKS,)),
                sem((CHUNKS,)),
                sem((CHUNKS,)),
                sem((CHUNKS,)),
                sem((zs,)),
                sem((zs,)),
                sem((batches, zs)),
                sem((batches, zs)),
                sem((zs,)),
                sem((zs,)),
            ],
            compiler_params=pltpu.CompilerParams(
                collective_id=0, has_side_effects=True, vmem_limit_bytes=60 * 1024 * 1024
            ),
        )(query_nope, query_rope, cache.T, key_docs.reshape(1, tokens), query_docs, query_pos, w_uk, w_uv)
        return out.astype(BF16)

    shared = P(("ga", "col"), None)
    flat = P(("ga", "col"))
    return jax.shard_map(
        shards,
        mesh=mesh,
        in_specs=(shared, shared, shared, flat, flat, flat, P(), P()),
        out_specs=shared,
        check_vma=False,
    )
```

```python
import functools
import math

import jax
import jax.numpy as jnp
from jax import lax
from jax.experimental import pallas as pl
from jax.experimental.pallas import tpu as pltpu
from jax.sharding import PartitionSpec as P

H = 32
DN = 128
DR = 64
DV = 128
R = 512
PLANE = 4
QUARTERS = 4
STEPS = H // QUARTERS
CHUNKS = 4
MESH = pl.DeviceIdType.MESH
F32 = jnp.float32
BF16 = jnp.bfloat16


def cut(rows):
    units = rows // 16
    ends = [16 * (units * i // CHUNKS) for i in range(CHUNKS + 1)]
    return [(a, b - a) for a, b in zip(ends[:-1], ends[1:])]


def split(x):
    high = x.astype(BF16)
    return high, (x - high.astype(F32)).astype(BF16)


def kernel(
    zs, batches, groups, nope_ref, rope_ref, cache_ref, kdocs_ref, qdocs_ref, qpos_ref, wuk_hbm, wuv_hbm, out_ref,
    wuk, wuv, kbuf, qtmp, qbuf, abuf, sbuf, pbuf, accb, obuf, rbuf, tbuf, trbuf,
    wsem, csend, crecv, xsend, xrecv, fsend, frecv, qsend, qrecv, osend, orecv, tsend, trecv,
):
    me = lax.axis_index("col")
    t = lax.rem(me, PLANE)
    zi = lax.div(me, PLANE)
    base = me - t
    mate_t = t + 1 - 2 * lax.rem(t, 2)
    cross_t = t + 2 - 4 * lax.div(t, 2)
    far_t = mate_t + 2 - 4 * lax.div(mate_t, 2)
    mate, cross = base + mate_t, base + cross_t
    peers = [lax.rem(zi + d, zs) * PLANE + t for d in range(zs)]

    barrier = pltpu.get_barrier_semaphore()
    for other in [mate, cross] + peers[1:]:
        pl.semaphore_signal(barrier, inc=1, device_id={"col": other}, device_id_type=MESH)

    load_uk = pltpu.make_async_copy(wuk_hbm, wuk, wsem.at[0])
    load_uv = pltpu.make_async_copy(wuv_hbm, wuv, wsem.at[1])
    load_uk.start()
    load_uv.start()

    tokens = cache_ref.shape[1]
    own = nope_ref.shape[0]
    rows = QUARTERS * own
    wide = STEPS * DN
    turn = STEPS * DR
    kbuf[0, :R + DR] = cache_ref[...]
    kbuf[0, R + DR:] = jnp.broadcast_to(kdocs_ref[...].astype(F32), (16, tokens)).astype(BF16)
    nope = nope_ref[...].astype(F32)
    rope = rope_ref[...].astype(F32)
    for k in range(QUARTERS):
        qtmp[pl.ds(own * k, own), :wide] = nope[:, k * wide:(k + 1) * wide]
        qtmp[pl.ds(own * k, own), wide:wide + turn] = rope[:, k * turn:(k + 1) * turn]
    row_query = lax.broadcasted_iota(jnp.int32, (rows, 128), 0) % own
    lane = lax.broadcasted_iota(jnp.int32, (rows, 128), 1)
    meta = jnp.zeros((rows, 128), jnp.int32)
    for i in range(own):
        place = qpos_ref[i]
        told = jnp.where(lane == 0, qdocs_ref[i], jnp.where(lane == 1, place >> 7, place & 127))
        meta = jnp.where(row_query == i, told, meta)
    qtmp[:, wide + turn:] = meta.astype(F32)
    qbuf[zi] = qtmp[...].astype(BF16)

    pl.semaphore_wait(barrier, 1 + zs)

    def remote(src, dst, send, recv, to):
        return pltpu.make_async_remote_copy(
            src_ref=src, dst_ref=dst, send_sem=send, recv_sem=recv, device_id={"col": to}, device_id_type=MESH
        )

    pieces = cut(R + DR + 16)
    x_copies = [
        remote(kbuf.at[0, pl.ds(a, n)], kbuf.at[2, pl.ds(a, n)], xsend.at[i], xrecv.at[i], cross)
        for i, (a, n) in enumerate(pieces)
    ]
    relays = [
        remote(kbuf.at[2, pl.ds(a, n)], kbuf.at[3, pl.ds(a, n)], fsend.at[i], frecv.at[i], mate)
        for i, (a, n) in enumerate(pieces)
    ]
    q_copies = [remote(qbuf.at[zi], qbuf.at[zi], qsend.at[d], qrecv.at[d], peers[d]) for d in range(1, zs)]
    mate_copy = remote(kbuf.at[0], kbuf.at[1], csend.at[0], crecv.at[0], mate)
    for c in x_copies:
        c.start()
    for c in q_copies:
        c.start()
    mate_copy.start()

    high_rows = zs * rows
    steps = STEPS // batches
    batch_rows = steps * high_rows
    group_steps = STEPS // groups
    group_rows = group_steps * high_rows
    quarter = lax.broadcasted_iota(jnp.int32, (high_rows, 128), 0) % rows // own
    pick = [quarter == k for k in range(QUARTERS)]
    pick_low = [jnp.where(p, 1.0, 0.0).astype(BF16) for p in pick]
    parity = lax.broadcasted_iota(jnp.int32, (high_rows, 128), 1) // DR
    side = [jnp.where(parity == i, 1.0, 0.0).astype(BF16) for i in range(2)]

    def relay(i):
        x_copies[i].wait_recv()
        relays[i].start()

    relay(0)
    relay(1)
    for c in q_copies:
        c.wait_recv()
    load_uk.wait()
    for h in range(STEPS):
        if h == STEPS // 2:
            relay(2)
        g, j = h // group_steps, h % group_steps
        q = qbuf[:, :, h * DN:(h + 1) * DN].reshape(high_rows, DN)
        spread = jnp.concatenate([q * p for p in pick_low], axis=1)
        w = jnp.concatenate([wuk[:, k * wide + h * DN:k * wide + (h + 1) * DN] for k in range(QUARTERS)], axis=1)
        absorbed = lax.dot_general(spread, w, (((1,), (1,)), ((), ())), preferred_element_type=F32)
        high, low = split(absorbed)
        at = wide + (h // 2) * 2 * DR
        turned = qbuf[:, :, at:at + 2 * DR].reshape(high_rows, 2 * DR) * side[h % 2]
        span = pl.ds(j * high_rows, high_rows)
        abuf[g, 0, span, :R] = high
        abuf[g, 1, span, :R] = low
        abuf[g, 0, span, R:] = turned
        abuf[g, 1, span, R:] = jnp.zeros_like(turned)

    told = qbuf[:, :, wide + turn:].reshape(high_rows, 128).astype(F32)
    q_doc = told[:, 0:1]
    q_place = told[:, 1:2] * 128.0 + told[:, 2:3]
    factor = math.log2(math.e) / math.sqrt(DN + DR)

    def score(slot, piece_t):
        k_doc = kbuf[slot, R + DR:, :].astype(F32)[0:1]
        first = (base + piece_t) * tokens
        k_place = (lax.broadcasted_iota(jnp.int32, (1, tokens), 1) + first).astype(F32)
        visible = (k_doc == q_doc) & (k_place <= q_place)
        keys = jnp.concatenate([kbuf[slot, :R + DR], kbuf[slot, R:R + DR]], axis=0)
        for g in range(groups):
            both = jnp.dot(abuf[g].reshape(2 * group_rows, R + 2 * DR), keys, preferred_element_type=F32)
            for j in range(group_steps):
                a = j * high_rows
                s = (both[a:a + high_rows] + both[group_rows + a:group_rows + a + high_rows]) * factor
                sbuf[g * group_steps + j, :, slot * tokens:(slot + 1) * tokens] = jnp.where(visible, s, -1e30)

    score(0, t)
    relay(3)
    mate_copy.wait_recv()
    score(1, mate_t)
    score(2, cross_t)
    for f in relays:
        f.wait_recv()
    score(3, far_t)

    stat_lane = lax.broadcasted_iota(jnp.int32, (high_rows, 128), 1)
    o_copies = []
    t_copies = []
    stats = jnp.zeros((high_rows, 128), F32)

    def weigh(b, stats):
        for j in range(steps):
            span = pl.ds(j * high_rows, high_rows)
            h = b * steps + j
            s = sbuf[h]
            top = jnp.max(s, axis=1, keepdims=True)
            p = jnp.exp2(s - top)
            total = jnp.sum(p, axis=1, keepdims=True)
            high, low = split(p)
            pbuf[b % 2, 0, span, :] = high
            pbuf[b % 2, 1, span, :] = low
            stats = jnp.where(stat_lane == h, top, jnp.where(stat_lane == 64 + h, total, stats))
        return stats

    load_uv.wait()
    stats = weigh(0, stats)
    for b in range(batches):
        if b < batches - 1:
            stats = weigh(b + 1, stats)
        if b == batches - 1:
            tbuf[...] = stats.reshape(zs, rows, 128)
            for d in range(1, zs):
                to = lax.rem(zi + d, zs)
                c = remote(tbuf.at[to], trbuf.at[d], tsend.at[d], trecv.at[d], peers[d])
                c.start()
                t_copies.append(c)
        mixed = jnp.zeros((2 * batch_rows, R), F32)
        for slot in range(PLANE):
            probs = pbuf[b % 2, :, :, slot * tokens:(slot + 1) * tokens].reshape(2 * batch_rows, tokens)
            mixed += lax.dot_general(
                probs, kbuf[slot, :R], (((1,), (1,)), ((), ())), preferred_element_type=F32
            )
        accb[...] = mixed[:batch_rows] + mixed[batch_rows:]
        for j in range(steps):
            h = b * steps + j
            high, low = split(accb[pl.ds(j * high_rows, high_rows), :])
            w = jnp.concatenate([wuv[:, k * wide + h * DV:k * wide + (h + 1) * DV] for k in range(QUARTERS)], axis=1)
            up = jnp.dot(jnp.concatenate([high, low], axis=0), w, preferred_element_type=F32)
            up = up[:high_rows] + up[high_rows:]
            mine = jnp.zeros((high_rows, DV), F32)
            for k in range(QUARTERS):
                mine = jnp.where(pick[k], up[:, k * DV:(k + 1) * DV], mine)
            obuf[b, :, :, j * DV:(j + 1) * DV] = mine.reshape(zs, rows, DV)
        for d in range(1, zs):
            to = lax.rem(zi + d, zs)
            c = remote(obuf.at[b, to], rbuf.at[b, d], osend.at[b, d], orecv.at[b, d], peers[d])
            c.start()
            o_copies.append(c)

    for c in t_copies:
        c.wait_recv()
    stats = [tbuf[zi]] + [trbuf[d] for d in range(1, zs)]
    top = functools.reduce(jnp.maximum, stats)
    share = [jnp.exp2(f - top) for f in stats]
    for b in range(batches):
        for c in o_copies[b * (zs - 1):(b + 1) * (zs - 1)]:
            c.wait_recv()
        found = [obuf[b, zi]] + [rbuf[b, d] for d in range(1, zs)]
        for j in range(steps):
            h = b * steps + j
            numer = jnp.zeros((rows, DV), F32)
            denom = jnp.zeros((rows, 1), F32)
            for f, s, w in zip(found, stats, share):
                part = w[:, h:h + 1]
                numer += part * f[:, j * DV:(j + 1) * DV]
                denom += part * s[:, 64 + h:65 + h]
            done = numer / denom
            for k in range(QUARTERS):
                out_ref[:, k * wide + h * DV:k * wide + (h + 1) * DV] = done[k * own:(k + 1) * own].astype(BF16)

    for c in [mate_copy] + x_copies + relays + q_copies + o_copies + t_copies:
        c.wait_send()


def solution(mesh):
    zs = mesh.shape["col"] // PLANE
    batches = 4 if zs <= 8 else 8
    groups = 1 if zs <= 8 else 8
    steps = STEPS // batches

    def shards(query_nope, query_rope, cache, key_docs, query_docs, query_pos, w_uk, w_uv):
        own = query_nope.shape[0]
        rows = QUARTERS * own
        tokens = cache.shape[0]
        payload = STEPS * (DN + DR) + 128
        high_rows = zs * rows
        batch_rows = steps * high_rows
        sem = pltpu.SemaphoreType.DMA
        vmem = pl.BlockSpec(memory_space=pltpu.VMEM)
        smem = pl.BlockSpec(memory_space=pltpu.SMEM)
        hbm = pl.BlockSpec(memory_space=pl.ANY)
        out = pl.pallas_call(
            functools.partial(kernel, zs, batches, groups),
            out_shape=jax.ShapeDtypeStruct((own, H * DV), BF16),
            in_specs=[vmem, vmem, vmem, vmem, smem, smem, hbm, hbm],
            out_specs=vmem,
            scratch_shapes=[
                pltpu.VMEM(w_uk.shape, BF16),
                pltpu.VMEM(w_uv.shape, BF16),
                pltpu.VMEM((PLANE, R + DR + 16, tokens), BF16),
                pltpu.VMEM((rows, payload), F32),
                pltpu.VMEM((zs, rows, payload), BF16),
                pltpu.VMEM((groups, 2, STEPS // groups * high_rows, R + 2 * DR), BF16),
                pltpu.VMEM((STEPS, high_rows, PLANE * tokens), F32),
                pltpu.VMEM((2, 2, batch_rows, PLANE * tokens), BF16),
                pltpu.VMEM((batch_rows, R), F32),
                pltpu.VMEM((batches, zs, rows, steps * DV), F32),
                pltpu.VMEM((batches, zs, rows, steps * DV), F32),
                pltpu.VMEM((zs, rows, 128), F32),
                pltpu.VMEM((zs, rows, 128), F32),
                sem((2,)),
                sem((1,)),
                sem((1,)),
                sem((CHUNKS,)),
                sem((CHUNKS,)),
                sem((CHUNKS,)),
                sem((CHUNKS,)),
                sem((zs,)),
                sem((zs,)),
                sem((batches, zs)),
                sem((batches, zs)),
                sem((zs,)),
                sem((zs,)),
            ],
            compiler_params=pltpu.CompilerParams(
                collective_id=0, has_side_effects=True, vmem_limit_bytes=60 * 1024 * 1024
            ),
        )(query_nope, query_rope, cache.T, key_docs.reshape(1, tokens), query_docs, query_pos, w_uk, w_uv)
        return out

    shared = P(("ga", "col"), None)
    flat = P(("ga", "col"))
    return jax.shard_map(
        shards,
        mesh=mesh,
        in_specs=(shared, shared, shared, flat, flat, flat, P(), P()),
        out_specs=shared,
        check_vma=False,
    )
```
